512 devices in a mesh: rep: 16 (over x, y_hi), fsdp: 32 (over z, y_lo, core).
Axes of the slice: x: 4, y: 8 (y_hi: 4, y_lo: 2; y = y_hi * 2 + y_lo), z: 8, core: 2. Of those that a mesh axis runs over, the one named last changes fastest.
Arguments:
- tokens: bfloat16 [16, 4096, 8192], P('rep', 'fsdp'), may hold values from -6 to 6
- cotangent: bfloat16 [16, 4096, 512], P('rep', 'fsdp'), may hold values from -6 to 6
- weight: bfloat16 [16, 8192, 512], P('rep', 'fsdp'), may hold values from -6 to 6
- moment: float32 [16, 8192, 512], P('rep', 'fsdp'), may hold values from -6 to 6
- global_frag: float32 [2, 8192, 128], P(None, 'fsdp'), may hold values from -6 to 6
- outer_moment: float32 [2, 8192, 128], P(None, 'fsdp'), may hold values from -3 to 3
- fragment: int32 [4], replicated, may hold values from 0 to 3, each once
Outputs:
- key_out: bfloat16 [16, 4096, 512], P('rep', 'fsdp')
- moment_new: float32 [16, 8192, 512], P('rep', 'fsdp')
- weight_new: bfloat16 [16, 8192, 512], P('rep', 'fsdp')
- global_new: float32 [2, 8192, 128], P(None, 'fsdp')
- outer_new: float32 [2, 8192, 128], P(None, 'fsdp')
The draws below stay inside these ranges and needn't reach their ends.
Inputs may be any that keep to these rules, and one draw needn't show every extreme that they name: `fragment`: each head appears once.
All inputs are finite; a program needn't handle non-finite values.
Results may differ from the reference program's by a relative error of at most 0.001.
Values may be sent and summed in bfloat16 or wider, within the bound.
No kernel may reach another device: no remote copies, remote signals or barrier semaphores. Data moves between devices by JAX's collectives and lax.ppermute only.
A program may use at most 64 MiB of HBM per device.

```python
import jax
import jax.numpy as jnp
from jax import lax

D = 8192
HD = 128
KVH = 4
TOKENS = 4096
REPLICAS = 16


def steps_of(key, shape, shards, smallest, top_value):
    level = 1.0
    for dim, blocks in shards:
        draws = jax.random.uniform(jax.random.fold_in(jax.random.fold_in(key, 6), dim), (blocks,), jnp.float32, smallest / len(shards), top_value / len(shards))
        level = level * jnp.repeat(jnp.exp(draws), shape[dim] // blocks).reshape((-1,) + (1,) * (len(shape) - 1 - dim))
    return level


def scatter_about(own_key, dims, spread, most, pieces=(), kind=jnp.bfloat16):
    result = spread * jax.random.normal(own_key, dims, jnp.float32)
    if pieces:
        result = result * steps_of(own_key, dims, pieces, -0.22, 0.18)
    return jnp.clip(result, -most, most).astype(kind)


def setup_inputs(seed: int = 0) -> dict:
    streams_of = jax.random.split(jax.random.key(seed), 8)
    return {
        "tokens": scatter_about(streams_of[0], (REPLICAS, TOKENS, D), 1.0, 6.0, ((0, 16), (1, 32))),
        "cotangent": scatter_about(streams_of[1], (REPLICAS, TOKENS, KVH * HD), 1.0, 6.0, ((0, 16), (1, 32))),
        "weight": scatter_about(streams_of[2], (REPLICAS, D, KVH * HD), 1.0, 6.0, ((0, 16), (1, 32))),
        "moment": scatter_about(streams_of[3], (REPLICAS, D, KVH * HD), 1.0, 6.0, ((0, 16), (1, 32)), jnp.float32),
        "global_frag": scatter_about(streams_of[4], (2, D, HD), 1.0, 6.0, ((1, 32),), jnp.float32),
        "outer_moment": scatter_about(streams_of[5], (2, D, HD), 0.5, 3.0, ((1, 32),), jnp.float32),
        "fragment": jax.random.permutation(streams_of[6], KVH).astype(jnp.int32),
    }


LR_INNER = 0.1
BETA_INNER = 0.9
MU_OUTER = 0.9
LR_OUTER = 0.7
ALPHA_MIX = 0.5


def replica_step(packed):
    tokens, cotangent, weight, moment = packed
    scale_factor = D ** -0.5
    key_sum = jnp.dot(tokens, weight, preferred_element_type=jnp.float32) * scale_factor
    gradient = lax.dot_general(tokens, cotangent, (((0,), (0,)), ((), ())), preferred_element_type=jnp.float32) * scale_factor
    moment_new = BETA_INNER * moment + gradient
    inner = weight.astype(jnp.float32) - LR_INNER * moment_new
    return key_sum.astype(jnp.bfloat16), moment_new, inner


def reference(tokens, cotangent, weight, moment, global_frag, outer_moment, fragment):
    key_out, moment_new, inner_all = lax.map(replica_step, (tokens, cotangent, weight, moment))
    head_first = fragment[0].astype(jnp.int32)
    head_second = fragment[1].astype(jnp.int32)
    prev_first = lax.dynamic_slice_in_dim(weight, head_first * HD, HD, 2).astype(jnp.float32)
    prev_second = lax.dynamic_slice_in_dim(weight, head_second * HD, HD, 2).astype(jnp.float32)
    previous = jnp.stack([prev_first, prev_second], axis=1)
    delta = global_frag[None] - previous
    mean_delta = jnp.sum(delta, axis=0) / REPLICAS
    outer_new = MU_OUTER * outer_moment + mean_delta
    global_new = global_frag - LR_OUTER * (MU_OUTER * outer_new + mean_delta)
    column_head = lax.broadcasted_iota(jnp.int32, (1, 1, KVH * HD), 2) // HD
    spread_first = jnp.tile(global_new[0], (1, KVH))[None]
    spread_second = jnp.tile(global_new[1], (1, KVH))[None]
    merged = jnp.where(column_head == head_first, ALPHA_MIX * inner_all + (1.0 - ALPHA_MIX) * spread_first,
                       jnp.where(column_head == head_second, ALPHA_MIX * inner_all + (1.0 - ALPHA_MIX) * spread_second, inner_all))
    return key_out, moment_new, merged.astype(jnp.bfloat16), global_new, outer_new
```

```python
import functools

import jax
import jax.numpy as jnp
from jax import lax
from jax.experimental import pallas as pl
from jax.experimental.pallas import tpu as pltpu
from jax.sharding import PartitionSpec as P

D = 8192
HD = 128
KVH = 4

LR_INNER = 0.1
BETA_INNER = 0.9
MU_OUTER = 0.9
LR_OUTER = 0.7
ALPHA_MIX = 0.5

F32 = jnp.float32
BF16 = jnp.bfloat16

NZ, NY, NC = 8, 2, 2
NG = NY * NC

ROWS = 256
TOK = 128
EARLY = (4, 3, -3)
LATE = (2, -2, 1, -1, 0)
DIST = EARLY + LATE
SPLIT = len(EARLY) * ROWS + KVH * HD
WIDE = SPLIT + len(LATE) * ROWS
LEVELS = 32000.0
CODED = ROWS + 16


def place(z, y, c):
    return ((z % NZ) * NY + y) * NC + c


def ring(dist):
    return [
        (place(z, y, c), place(z + (dist if c == 0 else -dist), y, c))
        for z in range(NZ) for y in range(NY) for c in range(NC)
    ]


def swap(k):
    return [(f, f ^ k) for f in range(NZ * NG)]


def z_groups():
    return [[place(z, y, c) for z in range(NZ)] for y in range(NY) for c in range(NC)]


def owner(dist, k=0):
    me = lax.axis_index("fsdp")
    z = me // NG
    forward = 1 - 2 * ((me % NC) ^ (k % NC))
    return (z + forward * dist + NZ) % NZ


def column_of(i):
    first = 0 if i < len(EARLY) else KVH * HD
    return first + i * ROWS


def piece_of(tok, i, k):
    me = lax.axis_index("fsdp")
    block = owner(DIST[i], k) * NG + ((me % NG) ^ k)
    return tok.at[:, pl.ds(pl.multiple_of(block * ROWS, ROWS), ROWS)]


def copy_all(pairs, sems):
    copies = [pltpu.make_async_copy(src, dst, sems.at[n]) for n, (src, dst) in enumerate(pairs)]
    for copy in copies:
        copy.start()
    for copy in copies:
        copy.wait()


def pack_early_kernel(tok, cot, y_early, x_early, near, sems):
    pairs = []
    for out, k in ((y_early, 2), (x_early, 3), (near, 1)):
        for i in range(len(DIST) if k == 1 else len(EARLY)):
            pairs.append((piece_of(tok, i, k), out.at[:, pl.ds(column_of(i), ROWS)]))
        pairs.append((cot, out.at[:, pl.ds(SPLIT - KVH * HD, KVH * HD)]))
    copy_all(pairs, sems)


def pack_late_kernel(frag, tok, cot, w, y_late, x_late, own, picked, sems):
    pairs = []
    for out, k in ((y_late, 2), (x_late, 3)):
        for i in range(len(EARLY), len(DIST)):
            pairs.append((piece_of(tok, i, k), out.at[:, pl.ds(column_of(i) - SPLIT, ROWS)]))
    for i in range(len(DIST)):
        pairs.append((piece_of(tok, i, 0), own.at[:, pl.ds(column_of(i), ROWS)]))
    pairs.append((cot, own.at[:, pl.ds(SPLIT - KVH * HD, KVH * HD)]))
    for k in range(2):
        src = w.at[:, pl.ds(pl.multiple_of(frag[k] * HD, HD), HD)]
        pairs.append((src, picked.at[:, pl.ds(k * HD, HD)]))
    copy_all(pairs, sems)


def encode(x, out):
    top = jnp.max(jnp.abs(x), axis=0, keepdims=True)
    power = jnp.ceil(jnp.log2(jnp.maximum(top, 1e-30)))
    out[:ROWS, :] = jnp.round(x * (LEVELS * jnp.exp2(-power))).astype(jnp.int32).astype(jnp.int16)
    out[ROWS:, :] = jnp.broadcast_to(power, (CODED - ROWS, x.shape[1])).astype(jnp.int32).astype(jnp.int16)


def decode(ref):
    power = ref[ROWS:, :].astype(jnp.int32).astype(F32)[0:1]
    return ref[:ROWS, :].astype(jnp.int32).astype(F32) * (jnp.exp2(power) * (1.0 / LEVELS))


def partial_grad(columns, cot):
    features = jnp.concatenate(columns, axis=0)
    return lax.dot_general(features, cot, (((0,), (0,)), ((), ())), preferred_element_type=F32)


def cotangents(refs):
    return jnp.concatenate([r[:, SPLIT - KVH * HD : SPLIT] for r in refs], axis=0)


def early_kernel(own, near, y_early, x_early, *outs):
    refs = (own, near, y_early, x_early)
    cot = cotangents(refs)
    for i, out in enumerate(outs):
        at = column_of(i)
        encode(partial_grad([r[:, at : at + ROWS] for r in refs], cot), out)


def late_columns(own, near, y_late, x_late, dist):
    at = column_of(DIST.index(dist))
    return [own[:, at : at + ROWS], near[:, at : at + ROWS],
            y_late[:, at - SPLIT : at - SPLIT + ROWS], x_late[:, at - SPLIT : at - SPLIT + ROWS]]


def next_kernel(own, near, y_early, x_early, y_late, x_late, ahead, behind, here):
    cot = cotangents((own, near, y_early, x_early))
    encode(partial_grad(late_columns(own, near, y_late, x_late, 1), cot), ahead)
    encode(partial_grad(late_columns(own, near, y_late, x_late, -1), cot), behind)
    here[...] = partial_grad(late_columns(own, near, y_late, x_late, 0), cot)


def relay_kernel(own, near, y_early, x_early, y_late, x_late, from4, from3, back3, ahead, behind):
    cot = cotangents((own, near, y_early, x_early))
    forward = partial_grad(late_columns(own, near, y_late, x_late, 2), cot)
    encode(forward + decode(from4) + decode(from3), ahead)
    backward = partial_grad(late_columns(own, near, y_late, x_late, -2), cot)
    encode(backward + decode(back3), behind)


def key_kernel(own, near, y_early, x_early, y_late, x_late, w, *outs):
    for k, (first, second) in enumerate(((own, None), (near, None), (y_early, y_late), (x_early, x_late))):
        total = jnp.zeros((TOK, KVH * HD), F32)
        for i, dist in enumerate(DIST):
            at = column_of(i)
            if second is None or at < SPLIT:
                piece = first[:, at : at + ROWS]
            else:
                piece = second[:, at - SPLIT : at - SPLIT + ROWS]
            rows = w[pl.ds(pl.multiple_of(owner(dist) * ROWS, ROWS), ROWS), :]
            total = total + jnp.dot(piece, rows, preferred_element_type=F32)
        outs[k][...] = total


def update_kernel(frag, here, ahead2, behind2, ahead1, behind1, w, moment, picked_sum, gf, om,
                  moment_new, weight_new, global_new, outer_new, *, replicas):
    grad = here[...] + decode(ahead2) + decode(behind2) + decode(ahead1) + decode(behind1)
    new = BETA_INNER * moment[...] + grad * (D ** -0.5)
    moment_new[...] = new
    inner = w[...].astype(F32) - LR_INNER * new
    for k in range(2):
        mean = gf[k] - picked_sum[:, k * HD : (k + 1) * HD] * (1.0 / replicas)
        out = MU_OUTER * om[k] + mean
        outer_new[k] = out
        global_new[k] = gf[k] - LR_OUTER * (MU_OUTER * out + mean)
    for h in range(KVH):
        mine = inner[:, h * HD : (h + 1) * HD]
        first = ALPHA_MIX * mine + (1.0 - ALPHA_MIX) * global_new[0]
        second = ALPHA_MIX * mine + (1.0 - ALPHA_MIX) * global_new[1]
        merged = jnp.where(frag[0] == h, first, jnp.where(frag[1] == h, second, mine))
        weight_new[:, h * HD : (h + 1) * HD] = merged.astype(BF16)


def key_sum_kernel(a, b, c, d, out):
    out[...] = ((a[...] + b[...] + c[...] + d[...]) * (D ** -0.5)).astype(BF16)


def call(kernel, outs, *args, flops=0, scalars=0, copies=0):
    moved = sum(a.size * a.dtype.itemsize for a in args)
    moved += sum(o.size * o.dtype.itemsize for o in outs)
    space = pl.ANY if copies else pltpu.VMEM
    specs = [pl.BlockSpec(memory_space=pltpu.SMEM)] * scalars
    specs += [pl.BlockSpec(memory_space=space)] * (len(args) - scalars)
    return pl.pallas_call(
        kernel,
        out_shape=list(outs),
        in_specs=specs,
        out_specs=[pl.BlockSpec(memory_space=pltpu.VMEM)] * len(outs),
        scratch_shapes=[pltpu.SemaphoreType.DMA((copies,))] if copies else [],
        compiler_params=None if copies else pltpu.CompilerParams(vmem_limit_bytes=24 * 2**20),
        cost_estimate=pl.CostEstimate(flops=0, bytes_accessed=0, transcendentals=0),
    )(*args)


def shape(*dims, kind=BF16):
    return jax.ShapeDtypeStruct(dims, kind)


def shards(tokens, cotangent, weight, moment, global_frag, outer_moment, fragment):
    replicas = lax.axis_size("rep")
    width = KVH * HD
    w = weight[0]
    w_rows = lax.all_gather(w, "fsdp", axis_index_groups=z_groups(), tiled=True)

    send = lambda x, pairs: lax.ppermute(x, "fsdp", pairs)
    y_early, x_early, near = call(
        pack_early_kernel, [shape(TOK, SPLIT)] * 2 + [shape(TOK, WIDE)], tokens[0], cotangent[0],
        copies=2 * len(EARLY) + len(DIST) + 3,
    )
    y_early = send(y_early, swap(2))
    x_early = send(x_early, swap(3))
    near = send(near, swap(1))
    y_late, x_late, own, picked = call(
        pack_late_kernel,
        [shape(TOK, WIDE - SPLIT)] * 2 + [shape(TOK, WIDE), shape(ROWS, 2 * HD)],
        fragment, tokens[0], cotangent[0], w, scalars=1, copies=2 * len(LATE) + len(DIST) + 3,
    )
    y_late = send(y_late, swap(2))
    x_late = send(x_late, swap(3))

    share = lax.all_to_all(picked.reshape(replicas, ROWS // replicas, 2 * HD), "rep", 0, 0)
    summed = jnp.sum(share.astype(F32), axis=0)
    coded = shape(CODED, width, kind=jnp.int16)
    block_flops = 2 * NG * TOK * ROWS * width
    to4, to3, back3 = call(early_kernel, [coded] * 3, own, near, y_early, x_early, flops=3 * block_flops)
    from4 = send(to4, ring(2))
    from3 = send(to3, ring(1))
    back3 = send(back3, ring(-1))

    got = (own, near, y_early, x_early, y_late, x_late)
    ahead1, behind1, here = call(
        next_kernel, [coded, coded, shape(ROWS, width, kind=F32)], *got, flops=3 * block_flops
    )
    picked_sum = lax.all_to_all(
        jnp.broadcast_to(summed[None], (replicas,) + summed.shape), "rep", 0, 0
    ).reshape(ROWS, 2 * HD)
    ahead1 = send(ahead1, ring(1))
    behind1 = send(behind1, ring(-1))
    ahead2, behind2 = call(relay_kernel, [coded] * 2, *got, from4, from3, back3, flops=2 * block_flops)
    ahead2 = send(ahead2, ring(2))
    behind2 = send(behind2, ring(-2))

    parts = call(key_kernel, [shape(TOK, width, kind=F32)] * NG, *got, w_rows, flops=8 * block_flops)
    (key_out,) = call(
        key_sum_kernel, [shape(TOK, width)], parts[0], *[send(parts[k], swap(k)) for k in range(1, NG)]
    )

    moment_new, weight_new, global_new, outer_new = call(
        functools.partial(update_kernel, replicas=replicas),
        [shape(ROWS, width, kind=F32), shape(ROWS, width), shape(2, ROWS, HD, kind=F32), shape(2, ROWS, HD, kind=F32)],
        fragment, here, ahead2, behind2, ahead1, behind1, w, moment[0], picked_sum, global_frag, outer_moment,
        scalars=1,
    )
    return key_out[None], moment_new[None], weight_new[None], global_new, outer_new


def solution(mesh):
    in_specs = (
        P("rep", "fsdp", None),
        P("rep", "fsdp", None),
        P("rep", "fsdp", None),
        P("rep", "fsdp", None),
        P(None, "fsdp", None),
        P(None, "fsdp", None),
        P(),
    )
    out_specs = (
        P("rep", "fsdp", None),
        P("rep", "fsdp", None),
        P("rep", "fsdp", None),
        P(None, "fsdp", None),
        P(None, "fsdp", None),
    )
    return jax.shard_map(shards, mesh=mesh, in_specs=in_specs, out_specs=out_specs, check_vma=False)
```

```python
import functools

import jax
import jax.numpy as jnp
from jax import lax
from jax.experimental import pallas as pl
from jax.experimental.pallas import tpu as pltpu
from jax.sharding import PartitionSpec as P

D = 8192
HD = 128
KVH = 4

LR_INNER = 0.1
BETA_INNER = 0.9
MU_OUTER = 0.9
LR_OUTER = 0.7
ALPHA_MIX = 0.5

F32 = jnp.float32
BF16 = jnp.bfloat16

NZ, NY, NC = 8, 2, 2
NX, NR = 4, 4
NG = NY * NC

ROWS = 256
TOK = 128
EARLY = (4, 3, 1, -3, -1)
LATE = (2, -2, 0)
DIST = EARLY + LATE
SPLIT = len(EARLY) * ROWS + KVH * HD
WIDE = SPLIT + len(LATE) * ROWS
LEVELS = 32000.0
CODED = ROWS + 16


def place(z, y, c):
    return ((z % NZ) * NY + y) * NC + c


def ring(dist):
    return [
        (place(z, y, c), place(z + (dist if c == 0 else -dist), y, c))
        for z in range(NZ) for y in range(NY) for c in range(NC)
    ]


def swap(k):
    return [(f, f ^ k) for f in range(NZ * NG)]


def z_groups():
    return [[place(z, y, c) for z in range(NZ)] for y in range(NY) for c in range(NC)]


def x_groups():
    return [[x * NR + y for x in range(NX)] for y in range(NR)]


def y_groups():
    return [[x * NR + y for y in range(NR)] for x in range(NX)]


def owner(dist, k=0):
    me = lax.axis_index("fsdp")
    z = me // NG
    forward = 1 - 2 * ((me % NC) ^ (k % NC))
    return (z + forward * dist + NZ) % NZ


def column_of(i):
    first = 0 if i < len(EARLY) else KVH * HD
    return first + i * ROWS


def piece_of(tok, i, k):
    me = lax.axis_index("fsdp")
    block = owner(DIST[i], k) * NG + ((me % NG) ^ k)
    return tok.at[:, pl.ds(pl.multiple_of(block * ROWS, ROWS), ROWS)]


def copy_all(pairs, sems):
    copies = [pltpu.make_async_copy(src, dst, sems.at[n]) for n, (src, dst) in enumerate(pairs)]
    for copy in copies:
        copy.start()
    for copy in copies:
        copy.wait()


def pack_early_kernel(tok, cot, y_early, x_early, near, sems):
    pairs = []
    for out, k in ((y_early, 2), (x_early, 3), (near, 1)):
        for i in range(len(DIST) if k == 1 else len(EARLY)):
            pairs.append((piece_of(tok, i, k), out.at[:, pl.ds(column_of(i), ROWS)]))
        pairs.append((cot, out.at[:, pl.ds(SPLIT - KVH * HD, KVH * HD)]))
    copy_all(pairs, sems)


def pack_late_kernel(frag, tok, cot, w, y_late, x_late, own, picked, sems):
    pairs = []
    for out, k in ((y_late, 2), (x_late, 3)):
        for i in range(len(EARLY), len(DIST)):
            pairs.append((piece_of(tok, i, k), out.at[:, pl.ds(column_of(i) - SPLIT, ROWS)]))
    for i in range(len(DIST)):
        pairs.append((piece_of(tok, i, 0), own.at[:, pl.ds(column_of(i), ROWS)]))
    pairs.append((cot, own.at[:, pl.ds(SPLIT - KVH * HD, KVH * HD)]))
    for k in range(2):
        src = w.at[:, pl.ds(pl.multiple_of(frag[k] * HD, HD), HD)]
        pairs += [(src, picked.at[n, :, pl.ds(k * HD, HD)]) for n in range(NX)]
    copy_all(pairs, sems)


def encode(x, out, at=0):
    top = jnp.max(jnp.abs(x), axis=0, keepdims=True)
    power = jnp.ceil(jnp.log2(jnp.maximum(top, 1e-30)))
    out[at : at + ROWS, :] = jnp.round(x * (LEVELS * jnp.exp2(-power))).astype(jnp.int32).astype(jnp.int16)
    out[at + ROWS : at + CODED, :] = (
        jnp.broadcast_to(power, (CODED - ROWS, x.shape[1])).astype(jnp.int32).astype(jnp.int16)
    )


def decode(ref, at=0):
    power = ref[at + ROWS : at + CODED, :].astype(jnp.int32).astype(F32)[0:1]
    return ref[at : at + ROWS, :].astype(jnp.int32).astype(F32) * (jnp.exp2(power) * (1.0 / LEVELS))


def partial_grad(refs, cot, dist):
    columns = [block_of(first, second, DIST.index(dist)) for first, second in refs]
    features = jnp.concatenate(columns, axis=0)
    return lax.dot_general(features, cot, (((0,), (0,)), ((), ())), preferred_element_type=F32)


def block_of(first, second, i):
    at = column_of(i)
    if second is None or at < SPLIT:
        return first[:, at : at + ROWS]
    return second[:, at - SPLIT : at - SPLIT + ROWS]


def cotangents(refs):
    return jnp.concatenate([r[:, SPLIT - KVH * HD : SPLIT] for r, _ in refs], axis=0)


def early_kernel(own, near, y_early, x_early, far, ahead, behind):
    refs = [(r, None) for r in (own, near, y_early, x_early)]
    cot = cotangents(refs)
    encode(partial_grad(refs, cot, 4), far)
    encode(partial_grad(refs, cot, 3), ahead)
    encode(partial_grad(refs, cot, 1), ahead, CODED)
    encode(partial_grad(refs, cot, -3), behind)
    encode(partial_grad(refs, cot, -1), behind, CODED)


def late_kernel(own, near, y_early, x_early, y_late, x_late, ahead2, behind2):
    refs = [(own, None), (near, None), (y_early, y_late), (x_early, x_late)]
    cot = cotangents(refs)
    ahead2[...] = partial_grad(refs, cot, 2)
    behind2[...] = partial_grad(refs, cot, -2)


def relay_kernel(mine_ahead, mine_behind, far, ahead, behind, ahead2, behind2):
    encode(mine_ahead[...] + decode(far) + decode(ahead), ahead2)
    encode(mine_behind[...] + decode(behind), behind2)


def key_kernel(own, near, y_early, x_early, y_late, x_late, w, moment, base, kept, sent):
    refs = [(own, None), (near, None), (y_early, y_late), (x_early, x_late)]
    for out, at, (first, second) in zip((kept, sent, kept, sent), (0, 0, TOK, TOK), refs):
        total = jnp.zeros((TOK, KVH * HD), F32)
        for i, dist in enumerate(DIST):
            rows = w[pl.ds(pl.multiple_of(owner(dist) * ROWS, ROWS), ROWS), :]
            total = total + jnp.dot(block_of(first, second, i), rows, preferred_element_type=F32)
        out[at : at + TOK, :] = total
    base[...] = BETA_INNER * moment[...] + partial_grad(refs, cotangents(refs), 0) * (D ** -0.5)


def picked_sum_kernel(picked, out):
    total = picked[0].astype(F32)
    for n in range(1, NX):
        total = total + picked[n].astype(F32)
    encode(total, out.at[0])
    for n in range(1, NR):
        out[n] = out[0]


def outer_kernel(sums, gf, om, global_new, outer_new, blend, *, replicas):
    total = decode(sums.at[0])
    for n in range(1, NR):
        total = total + decode(sums.at[n])
    for k in range(2):
        mean = gf[k] - total[:, k * HD : (k + 1) * HD] * (1.0 / replicas)
        out = MU_OUTER * om[k] + mean
        outer_new[k] = out
        new = gf[k] - LR_OUTER * (MU_OUTER * out + mean)
        global_new[k] = new
        blend[k] = (1.0 - ALPHA_MIX) * new


def update_kernel(frag, base, ahead2, behind2, ahead, behind, w, blend, moment_new, weight_new):
    others = decode(ahead2) + decode(behind2) + decode(ahead, CODED) + decode(behind, CODED)
    new = base[...] + others * (D ** -0.5)
    moment_new[...] = new
    inner = w[...].astype(F32) - LR_INNER * new
    for h in range(KVH):
        mine = inner[:, h * HD : (h + 1) * HD]
        first = ALPHA_MIX * mine + blend[0]
        second = ALPHA_MIX * mine + blend[1]
        merged = jnp.where(frag[0] == h, first, jnp.where(frag[1] == h, second, mine))
        weight_new[:, h * HD : (h + 1) * HD] = merged.astype(BF16)


def key_half_kernel(kept, got, mine, theirs):
    mine[...] = kept[:TOK, :] + got[:TOK, :]
    theirs[...] = kept[TOK:, :] + got[TOK:, :]


def key_sum_kernel(mine, got, out):
    out[...] = ((mine[...] + got[...]) * (D ** -0.5)).astype(BF16)


def call(kernel, outs, *args, scalars=0, copies=0, hint=0, first=False):
    space = pl.ANY if copies else pltpu.VMEM
    specs = [pl.BlockSpec(memory_space=pltpu.SMEM)] * scalars
    specs += [pl.BlockSpec(memory_space=space)] * (len(args) - scalars)
    return pl.pallas_call(
        kernel,
        out_shape=list(outs),
        in_specs=specs,
        out_specs=[pl.BlockSpec(memory_space=pltpu.VMEM)] * len(outs),
        scratch_shapes=[pltpu.SemaphoreType.DMA((copies,))] if copies else [],
        compiler_params=None if first else pltpu.CompilerParams(vmem_limit_bytes=16 * 2**20),
        cost_estimate=pl.CostEstimate(flops=hint * 10**9, bytes_accessed=0, transcendentals=0),
    )(*args)


def shape(*dims, kind=BF16):
    return jax.ShapeDtypeStruct(dims, kind)


def shards(tokens, cotangent, weight, moment, global_frag, outer_moment, fragment):
    replicas = lax.axis_size("rep")
    width = KVH * HD
    w = weight[0]
    w_rows = lax.all_gather(w, "fsdp", axis_index_groups=z_groups(), tiled=True)

    send = lambda x, pairs: lax.ppermute(x, "fsdp", pairs)
    y_early, x_early, near = call(
        pack_early_kernel, [shape(TOK, SPLIT)] * 2 + [shape(TOK, WIDE)], tokens[0], cotangent[0],
        copies=2 * len(EARLY) + len(DIST) + 3, first=True,
    )
    y_early = send(y_early, swap(2))
    x_early = send(x_early, swap(3))
    near = send(near, swap(1))
    y_late, x_late, own, picked = call(
        pack_late_kernel,
        [shape(TOK, WIDE - SPLIT)] * 2 + [shape(TOK, WIDE), shape(NX, ROWS, 2 * HD)],
        fragment, tokens[0], cotangent[0], w, scalars=1, copies=2 * len(LATE) + len(DIST) + 1 + 2 * NX,
    )
    y_late = send(y_late, swap(2))
    x_late = send(x_late, swap(3))

    picked = lax.all_to_all(picked, "rep", 0, 0, axis_index_groups=x_groups())

    one = shape(CODED, width, kind=jnp.int16)
    two = shape(2 * CODED, width, kind=jnp.int16)
    wide = shape(ROWS, width, kind=F32)
    far, ahead, behind = call(early_kernel, [one, two, two], own, near, y_early, x_early)
    far, y_late = lax.optimization_barrier((far, y_late))
    far = send(far, ring(2))
    ahead = send(ahead, ring(1))
    behind = send(behind, ring(-1))
    got = (own, near, y_early, x_early, y_late, x_late)
    mine = call(late_kernel, [wide] * 2, *got, hint=14)
    (sums,) = call(picked_sum_kernel, [shape(NR, CODED, 2 * HD, kind=jnp.int16)], picked)
    sums = lax.all_to_all(sums, "rep", 0, 0, axis_index_groups=y_groups())
    outer = shape(2, ROWS, HD, kind=F32)
    global_new, outer_new, blend = call(
        functools.partial(outer_kernel, replicas=replicas), [outer] * 3, sums, global_frag, outer_moment
    )
    pair = shape(2 * TOK, width, kind=F32)
    base, kept, sent = call(key_kernel, [wide, pair, pair], *got, w_rows, moment[0])
    half = shape(TOK, width, kind=F32)
    mine_key, theirs_key = call(key_half_kernel, [half] * 2, kept, send(sent, swap(1)))
    base, far = lax.optimization_barrier((base, far))
    ahead2, behind2 = call(relay_kernel, [one] * 2, *mine, far, ahead, behind)
    ahead2 = send(ahead2, ring(2))
    behind2 = send(behind2, ring(-2))
    (key_out,) = call(key_sum_kernel, [shape(TOK, width)], mine_key, send(theirs_key, swap(2)))

    moment_new, weight_new = call(
        update_kernel, [wide, shape(ROWS, width)],
        fragment, base, ahead2, behind2, ahead, behind, w, blend, scalars=1,
    )
    return key_out[None], moment_new[None], weight_new[None], global_new, outer_new


def solution(mesh):
    in_specs = (
        P("rep", "fsdp", None),
        P("rep", "fsdp", None),
        P("rep", "fsdp", None),
        P("rep", "fsdp", None),
        P(None, "fsdp", None),
        P(None, "fsdp", None),
        P(),
    )
    out_specs = (
        P("rep", "fsdp", None),
        P("rep", "fsdp", None),
        P("rep", "fsdp", None),
        P(None, "fsdp", None),
        P(None, "fsdp", None),
    )
    return jax.shard_map(shards, mesh=mesh, in_specs=in_specs, out_specs=out_specs, check_vma=False)
```

```python
import functools

import jax
import jax.numpy as jnp
from jax import lax
from jax.experimental import pallas as pl
from jax.experimental.pallas import tpu as pltpu
from jax.sharding import PartitionSpec as P

D = 8192
HD = 128
KVH = 4

LR_INNER = 0.1
BETA_INNER = 0.9
MU_OUTER = 0.9
LR_OUTER = 0.7
ALPHA_MIX = 0.5

F32 = jnp.float32
BF16 = jnp.bfloat16

NZ, NY, NC = 8, 2, 2
NX, NR = 4, 4
NG = NY * NC

ROWS = 256
TOK = 128
EARLY = (4, 3, 1, -3, -1)
LATE = (2, -2, 0)
DIST = EARLY + LATE
SPLIT = len(EARLY) * ROWS + KVH * HD
WIDE = SPLIT + len(LATE) * ROWS
LEVELS = 32000.0
CODED = ROWS + 16


def place(z, y, c):
    return ((z % NZ) * NY + y) * NC + c


def ring(dist):
    return [
        (place(z, y, c), place(z + (dist if c == 0 else -dist), y, c))
        for z in range(NZ) for y in range(NY) for c in range(NC)
    ]


def swap(k):
    return [(f, f ^ k) for f in range(NZ * NG)]


def z_groups():
    return [[place(z, y, c) for z in range(NZ)] for y in range(NY) for c in range(NC)]


def x_groups():
    return [[x * NR + y for x in range(NX)] for y in range(NR)]


def y_groups():
    return [[x * NR + y for y in range(NR)] for x in range(NX)]


def owner(dist, k=0):
    me = lax.axis_index("fsdp")
    z = me // NG
    forward = 1 - 2 * ((me % NC) ^ (k % NC))
    return (z + forward * dist + NZ) % NZ


def column_of(i):
    first = 0 if i < len(EARLY) else KVH * HD
    return first + i * ROWS


def piece_of(tok, i, k):
    me = lax.axis_index("fsdp")
    block = owner(DIST[i], k) * NG + ((me % NG) ^ k)
    return tok.at[:, pl.ds(pl.multiple_of(block * ROWS, ROWS), ROWS)]


def copy_all(pairs, sems):
    copies = [pltpu.make_async_copy(src, dst, sems.at[n]) for n, (src, dst) in enumerate(pairs)]
    for copy in copies:
        copy.start()
    for copy in copies:
        copy.wait()


def pack_early_kernel(tok, cot, y_early, x_early, near, sems):
    pairs = []
    for out, k in ((y_early, 2), (x_early, 3), (near, 1)):
        for i in range(len(DIST) if k == 1 else len(EARLY)):
            pairs.append((piece_of(tok, i, k), out.at[:, pl.ds(column_of(i), ROWS)]))
        pairs.append((cot, out.at[:, pl.ds(SPLIT - KVH * HD, KVH * HD)]))
    copy_all(pairs, sems)


def pack_late_kernel(tok, cot, y_late, x_late, own, sems):
    pairs = []
    for out, k in ((y_late, 2), (x_late, 3)):
        for i in range(len(EARLY), len(DIST)):
            pairs.append((piece_of(tok, i, k), out.at[:, pl.ds(column_of(i) - SPLIT, ROWS)]))
    for i in range(len(DIST)):
        pairs.append((piece_of(tok, i, 0), own.at[:, pl.ds(column_of(i), ROWS)]))
    pairs.append((cot, own.at[:, pl.ds(SPLIT - KVH * HD, KVH * HD)]))
    copy_all(pairs, sems)


def pick_kernel(frag, w, picked, sems):
    pairs = []
    for k in range(2):
        src = w.at[:, pl.ds(pl.multiple_of(frag[k] * HD, HD), HD)]
        pairs += [(src, picked.at[n, :, pl.ds(k * HD, HD)]) for n in range(NX)]
    copy_all(pairs, sems)


def encode(x, out, at=0):
    top = jnp.max(jnp.abs(x), axis=0, keepdims=True)
    power = jnp.ceil(jnp.log2(jnp.maximum(top, 1e-30)))
    out[at : at + ROWS, :] = jnp.round(x * (LEVELS * jnp.exp2(-power))).astype(jnp.int32).astype(jnp.int16)
    out[at + ROWS : at + CODED, :] = (
        jnp.broadcast_to(power, (CODED - ROWS, x.shape[1])).astype(jnp.int32).astype(jnp.int16)
    )


def decode(ref, at=0):
    power = ref[at + ROWS : at + CODED, :].astype(jnp.int32).astype(F32)[0:1]
    return ref[at : at + ROWS, :].astype(jnp.int32).astype(F32) * (jnp.exp2(power) * (1.0 / LEVELS))


def partial_grad(refs, cot, dist):
    columns = [block_of(first, second, DIST.index(dist)) for first, second in refs]
    features = jnp.concatenate(columns, axis=0)
    return lax.dot_general(features, cot, (((0,), (0,)), ((), ())), preferred_element_type=F32)


def block_of(first, second, i):
    at = column_of(i)
    if second is None or at < SPLIT:
        return first[:, at : at + ROWS]
    return second[:, at - SPLIT : at - SPLIT + ROWS]


def cotangents(refs):
    return jnp.concatenate([r[:, SPLIT - KVH * HD : SPLIT] for r, _ in refs], axis=0)


def early_kernel(own, near, y_early, x_early, far, ahead, behind):
    refs = [(r, None) for r in (own, near, y_early, x_early)]
    cot = cotangents(refs)
    encode(partial_grad(refs, cot, 4), far)
    encode(partial_grad(refs, cot, 3), ahead)
    encode(partial_grad(refs, cot, 1), ahead, CODED)
    encode(partial_grad(refs, cot, -3), behind)
    encode(partial_grad(refs, cot, -1), behind, CODED)


def late_kernel(own, near, y_early, x_early, y_late, x_late, ahead2, behind2):
    refs = [(own, None), (near, None), (y_early, y_late), (x_early, x_late)]
    cot = cotangents(refs)
    ahead2[...] = partial_grad(refs, cot, 2)
    behind2[...] = partial_grad(refs, cot, -2)


def relay_kernel(mine_ahead, mine_behind, far, ahead, behind, ahead2, behind2):
    encode(mine_ahead[...] + decode(far) + decode(ahead), ahead2)
    encode(mine_behind[...] + decode(behind), behind2)


def key_kernel(own, near, y_early, x_early, y_late, x_late, w, moment, base, kept, sent):
    refs = [(own, None), (near, None), (y_early, y_late), (x_early, x_late)]
    for out, at, (first, second) in zip((kept, sent, kept, sent), (0, 0, TOK, TOK), refs):
        total = jnp.zeros((TOK, KVH * HD), F32)
        for i, dist in enumerate(DIST):
            rows = w[pl.ds(pl.multiple_of(owner(dist) * ROWS, ROWS), ROWS), :]
            total = total + jnp.dot(block_of(first, second, i), rows, preferred_element_type=F32)
        out[at : at + TOK, :] = total
    base[...] = BETA_INNER * moment[...] + partial_grad(refs, cotangents(refs), 0) * (D ** -0.5)


def picked_sum_kernel(picked, out):
    total = picked[0].astype(F32)
    for n in range(1, NX):
        total = total + picked[n].astype(F32)
    encode(total, out.at[0])
    for n in range(1, NR):
        out[n] = out[0]


def outer_kernel(sums, gf, om, global_new, outer_new, blend, *, replicas):
    total = decode(sums.at[0])
    for n in range(1, NR):
        total = total + decode(sums.at[n])
    for k in range(2):
        mean = gf[k] - total[:, k * HD : (k + 1) * HD] * (1.0 / replicas)
        out = MU_OUTER * om[k] + mean
        outer_new[k] = out
        new = gf[k] - LR_OUTER * (MU_OUTER * out + mean)
        global_new[k] = new
        blend[k] = (1.0 - ALPHA_MIX) * new


def update_kernel(frag, base, ahead2, behind2, ahead, behind, w, blend, moment_new, weight_new):
    others = decode(ahead2) + decode(behind2) + decode(ahead, CODED) + decode(behind, CODED)
    new = base[...] + others * (D ** -0.5)
    moment_new[...] = new
    inner = w[...].astype(F32) - LR_INNER * new
    for h in range(KVH):
        mine = inner[:, h * HD : (h + 1) * HD]
        first = ALPHA_MIX * mine + blend[0]
        second = ALPHA_MIX * mine + blend[1]
        merged = jnp.where(frag[0] == h, first, jnp.where(frag[1] == h, second, mine))
        weight_new[:, h * HD : (h + 1) * HD] = merged.astype(BF16)


def key_half_kernel(kept, got, mine, theirs):
    mine[...] = kept[:TOK, :] + got[:TOK, :]
    theirs[...] = kept[TOK:, :] + got[TOK:, :]


def key_sum_kernel(mine, got, out):
    out[...] = ((mine[...] + got[...]) * (D ** -0.5)).astype(BF16)


def call(kernel, outs, *args, scalars=0, copies=0, hint=0, first=False):
    space = pl.ANY if copies else pltpu.VMEM
    specs = [pl.BlockSpec(memory_space=pltpu.SMEM)] * scalars
    specs += [pl.BlockSpec(memory_space=space)] * (len(args) - scalars)
    return pl.pallas_call(
        kernel,
        out_shape=list(outs),
        in_specs=specs,
        out_specs=[pl.BlockSpec(memory_space=pltpu.VMEM)] * len(outs),
        scratch_shapes=[pltpu.SemaphoreType.DMA((copies,))] if copies else [],
        compiler_params=None if first else pltpu.CompilerParams(vmem_limit_bytes=16 * 2**20),
        cost_estimate=pl.CostEstimate(flops=hint * 10**9, bytes_accessed=0, transcendentals=0),
    )(*args)


def shape(*dims, kind=BF16):
    return jax.ShapeDtypeStruct(dims, kind)


def shards(tokens, cotangent, weight, moment, global_frag, outer_moment, fragment):
    replicas = lax.axis_size("rep")
    width = KVH * HD
    w = weight[0]
    w_rows = lax.all_gather(w, "fsdp", axis_index_groups=z_groups(), tiled=True)

    send = lambda x, pairs: lax.ppermute(x, "fsdp", pairs)
    y_early, x_early, near = call(
        pack_early_kernel, [shape(TOK, SPLIT)] * 2 + [shape(TOK, WIDE)], tokens[0], cotangent[0],
        copies=2 * len(EARLY) + len(DIST) + 3, first=True,
    )
    y_early = send(y_early, swap(2))
    x_early = send(x_early, swap(3))
    near = send(near, swap(1))
    (picked,) = call(pick_kernel, [shape(NX, ROWS, 2 * HD)], fragment, w, scalars=1, copies=2 * NX)
    y_late, x_late, own = call(
        pack_late_kernel, [shape(TOK, WIDE - SPLIT)] * 2 + [shape(TOK, WIDE)],
        tokens[0], cotangent[0], copies=2 * len(LATE) + len(DIST) + 1,
    )
    y_late = send(y_late, swap(2))
    x_late = send(x_late, swap(3))

    picked = lax.all_to_all(picked, "rep", 0, 0, axis_index_groups=x_groups())

    one = shape(CODED, width, kind=jnp.int16)
    two = shape(2 * CODED, width, kind=jnp.int16)
    wide = shape(ROWS, width, kind=F32)
    far, ahead, behind = call(early_kernel, [one, two, two], own, near, y_early, x_early)
    far, y_late = lax.optimization_barrier((far, y_late))
    far = send(far, ring(2))
    ahead = send(ahead, ring(1))
    behind = send(behind, ring(-1))
    got = (own, near, y_early, x_early, y_late, x_late)
    mine = call(late_kernel, [wide] * 2, *got, hint=14)
    (sums,) = call(picked_sum_kernel, [shape(NR, CODED, 2 * HD, kind=jnp.int16)], picked)
    sums = lax.all_to_all(sums, "rep", 0, 0, axis_index_groups=y_groups())
    outer = shape(2, ROWS, HD, kind=F32)
    global_new, outer_new, blend = call(
        functools.partial(outer_kernel, replicas=replicas), [outer] * 3, sums, global_frag, outer_moment
    )
    pair = shape(2 * TOK, width, kind=F32)
    base, kept, sent = call(key_kernel, [wide, pair, pair], *got, w_rows, moment[0])
    half = shape(TOK, width, kind=F32)
    mine_key, theirs_key = call(key_half_kernel, [half] * 2, kept, send(sent, swap(1)))
    base, far = lax.optimization_barrier((base, far))
    ahead2, behind2 = call(relay_kernel, [one] * 2, *mine, far, ahead, behind)
    ahead2 = send(ahead2, ring(2))
    behind2 = send(behind2, ring(-2))
    (key_out,) = call(key_sum_kernel, [shape(TOK, width)], mine_key, send(theirs_key, swap(2)))

    moment_new, weight_new = call(
        update_kernel, [wide, shape(ROWS, width)],
        fragment, base, ahead2, behind2, ahead, behind, w, blend, scalars=1,
    )
    return key_out[None], moment_new[None], weight_new[None], global_new, outer_new


def solution(mesh):
    in_specs = (
        P("rep", "fsdp", None),
        P("rep", "fsdp", None),
        P("rep", "fsdp", None),
        P("rep", "fsdp", None),
        P(None, "fsdp", None),
        P(None, "fsdp", None),
        P(),
    )
    out_specs = (
        P("rep", "fsdp", None),
        P("rep", "fsdp", None),
        P("rep", "fsdp", None),
        P(None, "fsdp", None),
        P(None, "fsdp", None),
    )
    return jax.shard_map(shards, mesh=mesh, in_specs=in_specs, out_specs=out_specs, check_vma=False)
```

```python
import functools

import jax
import jax.numpy as jnp
from jax import lax
from jax.experimental import pallas as pl
from jax.experimental.pallas import tpu as pltpu
from jax.sharding import PartitionSpec as P

D = 8192
HD = 128
KVH = 4

LR_INNER = 0.1
BETA_INNER = 0.9
MU_OUTER = 0.9
LR_OUTER = 0.7
ALPHA_MIX = 0.5

F32 = jnp.float32
BF16 = jnp.bfloat16

NZ, NY, NC = 8, 2, 2
NX, NR = 4, 4
NG = NY * NC

ROWS = 256
TOK = 128
EARLY = (4, 3, 1, -3, -1)
LATE = (2, -2, 0)
DIST = EARLY + LATE
SPLIT = len(EARLY) * ROWS + KVH * HD
WIDE = SPLIT + len(LATE) * ROWS
LEVELS = 32000.0
GROUP = 16
CODED = ROWS + GROUP


def place(z, y, c):
    return ((z % NZ) * NY + y) * NC + c


def ring(dist):
    return [
        (place(z, y, c), place(z + (dist if c == 0 else -dist), y, c))
        for z in range(NZ) for y in range(NY) for c in range(NC)
    ]


def swap(k):
    return [(f, f ^ k) for f in range(NZ * NG)]


def z_groups():
    return [[place(z, y, c) for z in range(NZ)] for y in range(NY) for c in range(NC)]


def x_groups():
    return [[x * NR + y for x in range(NX)] for y in range(NR)]


def y_groups():
    return [[x * NR + y for y in range(NR)] for x in range(NX)]


def owner(dist, k=0):
    me = lax.axis_index("fsdp")
    z = me // NG
    forward = 1 - 2 * ((me % NC) ^ (k % NC))
    return (z + forward * dist + NZ) % NZ


def column_of(i):
    first = 0 if i < len(EARLY) else KVH * HD
    return first + i * ROWS


def piece_of(tok, i, k):
    me = lax.axis_index("fsdp")
    block = owner(DIST[i], k) * NG + ((me % NG) ^ k)
    return tok.at[:, pl.ds(pl.multiple_of(block * ROWS, ROWS), ROWS)]


def copy_all(pairs, sems):
    copies = [pltpu.make_async_copy(src, dst, sems.at[n]) for n, (src, dst) in enumerate(pairs)]
    for copy in copies:
        copy.start()
    for copy in copies:
        copy.wait()


def pack_early_kernel(tok, cot, y_early, x_early, near, sems):
    pairs = []
    for out, k in ((y_early, 2), (x_early, 3), (near, 1)):
        for i in range(len(DIST) if k == 1 else len(EARLY)):
            pairs.append((piece_of(tok, i, k), out.at[:, pl.ds(column_of(i), ROWS)]))
        pairs.append((cot, out.at[:, pl.ds(SPLIT - KVH * HD, KVH * HD)]))
    copy_all(pairs, sems)


def pack_late_kernel(tok, cot, y_late, x_late, own, sems):
    pairs = []
    for out, k in ((y_late, 2), (x_late, 3)):
        for i in range(len(EARLY), len(DIST)):
            pairs.append((piece_of(tok, i, k), out.at[:, pl.ds(column_of(i) - SPLIT, ROWS)]))
    for i in range(len(DIST)):
        pairs.append((piece_of(tok, i, 0), own.at[:, pl.ds(column_of(i), ROWS)]))
    pairs.append((cot, own.at[:, pl.ds(SPLIT - KVH * HD, KVH * HD)]))
    copy_all(pairs, sems)


def pick_kernel(frag, w, picked, sems):
    pairs = []
    for k in range(2):
        src = w.at[:, pl.ds(pl.multiple_of(frag[k] * HD, HD), HD)]
        pairs += [(src, picked.at[n, :, pl.ds(k * HD, HD)]) for n in range(NX)]
    copy_all(pairs, sems)


def levels_of(x):
    top = jnp.max(jnp.abs(x), axis=0, keepdims=True)
    power = jnp.ceil(jnp.log2(jnp.maximum(top, 1e-30)))
    return jnp.round(x * (LEVELS * jnp.exp2(-power))).astype(jnp.int32).astype(jnp.int16), power


def encode(x, out):
    coded, power = levels_of(x)
    out[:ROWS, :] = coded
    out[ROWS:, :] = jnp.broadcast_to(power, (GROUP, x.shape[1])).astype(jnp.int32).astype(jnp.int16)


def encode_pair(x, y, out):
    coded_x, power_x = levels_of(x)
    coded_y, power_y = levels_of(y)
    out[:ROWS, :] = coded_x
    out[ROWS : 2 * ROWS, :] = coded_y
    half = (GROUP // 2, x.shape[1])
    powers = jnp.concatenate([jnp.broadcast_to(power_x, half), jnp.broadcast_to(power_y, half)], axis=0)
    out[2 * ROWS :, :] = powers.astype(jnp.int32).astype(jnp.int16)


def decode(ref, at=0, blocks=1):
    powers = ref[blocks * ROWS :, :].astype(jnp.int32).astype(F32)
    row = at * (GROUP // blocks)
    scale = jnp.exp2(powers[row : row + 1]) * (1.0 / LEVELS)
    return ref[at * ROWS : (at + 1) * ROWS, :].astype(jnp.int32).astype(F32) * scale


def partial_grad(refs, cot, dist):
    columns = [block_of(first, second, DIST.index(dist)) for first, second in refs]
    features = jnp.concatenate(columns, axis=0)
    return lax.dot_general(features, cot, (((0,), (0,)), ((), ())), preferred_element_type=F32)


def block_of(first, second, i):
    at = column_of(i)
    if second is None or at < SPLIT:
        return first[:, at : at + ROWS]
    return second[:, at - SPLIT : at - SPLIT + ROWS]


def cotangents(refs):
    return jnp.concatenate([r[:, SPLIT - KVH * HD : SPLIT] for r, _ in refs], axis=0)


def early_kernel(own, near, y_early, x_early, far, ahead, behind):
    refs = [(r, None) for r in (own, near, y_early, x_early)]
    cot = cotangents(refs)
    encode(partial_grad(refs, cot, 4), far)
    encode_pair(partial_grad(refs, cot, 3), partial_grad(refs, cot, 1), ahead)
    encode_pair(partial_grad(refs, cot, -3), partial_grad(refs, cot, -1), behind)


def late_kernel(own, near, y_early, x_early, y_late, x_late, ahead2, behind2):
    refs = [(own, None), (near, None), (y_early, y_late), (x_early, x_late)]
    cot = cotangents(refs)
    ahead2[...] = partial_grad(refs, cot, 2)
    behind2[...] = partial_grad(refs, cot, -2)


def relay_kernel(mine_ahead, mine_behind, far, ahead, behind, ahead2, behind2):
    encode(mine_ahead[...] + decode(far) + decode(ahead, 0, 2), ahead2)
    encode(mine_behind[...] + decode(behind, 0, 2), behind2)


def key_kernel(own, near, y_early, x_early, y_late, x_late, w, moment, base, kept, sent):
    refs = [(own, None), (near, None), (y_early, y_late), (x_early, x_late)]
    for out, at, (first, second) in zip((kept, sent, kept, sent), (0, 0, TOK, TOK), refs):
        total = jnp.zeros((TOK, KVH * HD), F32)
        for i, dist in enumerate(DIST):
            rows = w[pl.ds(pl.multiple_of(owner(dist) * ROWS, ROWS), ROWS), :]
            total = total + jnp.dot(block_of(first, second, i), rows, preferred_element_type=F32)
        out[at : at + TOK, :] = total
    base[...] = BETA_INNER * moment[...] + partial_grad(refs, cotangents(refs), 0) * (D ** -0.5)


def picked_sum_kernel(picked, out):
    total = picked[0].astype(F32)
    for n in range(1, NX):
        total = total + picked[n].astype(F32)
    encode(total, out.at[0])
    for n in range(1, NR):
        out[n] = out[0]


def outer_kernel(sums, gf, om, global_new, outer_new, blend, *, replicas):
    total = decode(sums.at[0])
    for n in range(1, NR):
        total = total + decode(sums.at[n])
    for k in range(2):
        mean = gf[k] - total[:, k * HD : (k + 1) * HD] * (1.0 / replicas)
        out = MU_OUTER * om[k] + mean
        outer_new[k] = out
        new = gf[k] - LR_OUTER * (MU_OUTER * out + mean)
        global_new[k] = new
        blend[k] = (1.0 - ALPHA_MIX) * new


def update_kernel(frag, base, ahead2, behind2, ahead, behind, w, blend, moment_new, weight_new):
    others = decode(ahead2) + decode(behind2) + decode(ahead, 1, 2) + decode(behind, 1, 2)
    new = base[...] + others * (D ** -0.5)
    moment_new[...] = new
    inner = w[...].astype(F32) - LR_INNER * new
    for h in range(KVH):
        mine = inner[:, h * HD : (h + 1) * HD]
        first = ALPHA_MIX * mine + blend[0]
        second = ALPHA_MIX * mine + blend[1]
        merged = jnp.where(frag[0] == h, first, jnp.where(frag[1] == h, second, mine))
        weight_new[:, h * HD : (h + 1) * HD] = merged.astype(BF16)


def key_half_kernel(kept, got, mine, theirs):
    mine[...] = kept[:TOK, :] + got[:TOK, :]
    theirs[...] = kept[TOK:, :] + got[TOK:, :]


def key_sum_kernel(mine, got, out):
    out[...] = ((mine[...] + got[...]) * (D ** -0.5)).astype(BF16)


def call(kernel, outs, *args, scalars=0, copies=0, hint=0, first=False):
    space = pl.ANY if copies else pltpu.VMEM
    specs = [pl.BlockSpec(memory_space=pltpu.SMEM)] * scalars
    specs += [pl.BlockSpec(memory_space=space)] * (len(args) - scalars)
    return pl.pallas_call(
        kernel,
        out_shape=list(outs),
        in_specs=specs,
        out_specs=[pl.BlockSpec(memory_space=pltpu.VMEM)] * len(outs),
        scratch_shapes=[pltpu.SemaphoreType.DMA((copies,))] if copies else [],
        compiler_params=None if first else pltpu.CompilerParams(vmem_limit_bytes=16 * 2**20),
        cost_estimate=pl.CostEstimate(flops=hint * 10**9, bytes_accessed=0, transcendentals=0),
    )(*args)


def shape(*dims, kind=BF16):
    return jax.ShapeDtypeStruct(dims, kind)


def shards(tokens, cotangent, weight, moment, global_frag, outer_moment, fragment):
    replicas = lax.axis_size("rep")
    width = KVH * HD
    w = weight[0]
    w_rows = lax.all_gather(w, "fsdp", axis_index_groups=z_groups(), tiled=True)

    send = lambda x, pairs: lax.ppermute(x, "fsdp", pairs)
    y_early, x_early, near = call(
        pack_early_kernel, [shape(TOK, SPLIT)] * 2 + [shape(TOK, WIDE)], tokens[0], cotangent[0],
        copies=2 * len(EARLY) + len(DIST) + 3, first=True,
    )
    y_early = send(y_early, swap(2))
    x_early = send(x_early, swap(3))
    near = send(near, swap(1))
    (picked,) = call(pick_kernel, [shape(NX, ROWS, 2 * HD)], fragment, w, scalars=1, copies=2 * NX)
    y_late, x_late, own = call(
        pack_late_kernel, [shape(TOK, WIDE - SPLIT)] * 2 + [shape(TOK, WIDE)],
        tokens[0], cotangent[0], copies=2 * len(LATE) + len(DIST) + 1,
    )
    y_late = send(y_late, swap(2))
    x_late = send(x_late, swap(3))

    picked = lax.all_to_all(picked, "rep", 0, 0, axis_index_groups=x_groups())

    one = shape(CODED, width, kind=jnp.int16)
    two = shape(2 * ROWS + GROUP, width, kind=jnp.int16)
    wide = shape(ROWS, width, kind=F32)
    far, ahead, behind = call(early_kernel, [one, two, two], own, near, y_early, x_early)
    far, y_late = lax.optimization_barrier((far, y_late))
    far = send(far, ring(2))
    ahead = send(ahead, ring(1))
    behind = send(behind, ring(-1))
    got = (own, near, y_early, x_early, y_late, x_late)
    mine = call(late_kernel, [wide] * 2, *got, hint=14)
    (sums,) = call(picked_sum_kernel, [shape(NR, CODED, 2 * HD, kind=jnp.int16)], picked)
    sums = lax.all_to_all(sums, "rep", 0, 0, axis_index_groups=y_groups())
    outer = shape(2, ROWS, HD, kind=F32)
    global_new, outer_new, blend = call(
        functools.partial(outer_kernel, replicas=replicas), [outer] * 3, sums, global_frag, outer_moment
    )
    pair = shape(2 * TOK, width, kind=F32)
    base, kept, sent = call(key_kernel, [wide, pair, pair], *got, w_rows, moment[0])
    half = shape(TOK, width, kind=F32)
    mine_key, theirs_key = call(key_half_kernel, [half] * 2, kept, send(sent, swap(1)))
    base, far = lax.optimization_barrier((base, far))
    ahead2, behind2 = call(relay_kernel, [one] * 2, *mine, far, ahead, behind, hint=12)
    ahead2 = send(ahead2, ring(2))
    behind2 = send(behind2, ring(-2))
    (key_out,) = call(key_sum_kernel, [shape(TOK, width)], mine_key, send(theirs_key, swap(2)))

    moment_new, weight_new = call(
        update_kernel, [wide, shape(ROWS, width)],
        fragment, base, ahead2, behind2, ahead, behind, w, blend, scalars=1,
    )
    return key_out[None], moment_new[None], weight_new[None], global_new, outer_new


def solution(mesh):
    in_specs = (
        P("rep", "fsdp", None),
        P("rep", "fsdp", None),
        P("rep", "fsdp", None),
        P("rep", "fsdp", None),
        P(None, "fsdp", None),
        P(None, "fsdp", None),
        P(),
    )
    out_specs = (
        P("rep", "fsdp", None),
        P("rep", "fsdp", None),
        P("rep", "fsdp", None),
        P(None, "fsdp", None),
        P(None, "fsdp", None),
    )
    return jax.shard_map(shards, mesh=mesh, in_specs=in_specs, out_specs=out_specs, check_vma=False)
```

```python
import functools

import jax
import jax.numpy as jnp
from jax import lax
from jax.experimental import pallas as pl
from jax.experimental.pallas import tpu as pltpu
from jax.sharding import PartitionSpec as P

D = 8192
HD = 128
KVH = 4

LR_INNER = 0.1
BETA_INNER = 0.9
MU_OUTER = 0.9
LR_OUTER = 0.7
ALPHA_MIX = 0.5

F32 = jnp.float32
BF16 = jnp.bfloat16

NZ, NY, NC = 8, 2, 2
NX, NR = 4, 4
NG = NY * NC

ROWS = 256
TOK = 128
EARLY = (4, 3, 1, -3, -1)
LATE = (2, -2, 0)
DIST = EARLY + LATE
SPLIT = len(EARLY) * ROWS + KVH * HD
WIDE = SPLIT + len(LATE) * ROWS
LEVELS = 32000.0
GROUP = 16
CODED = ROWS + GROUP


def place(z, y, c):
    return ((z % NZ) * NY + y) * NC + c


def ring(dist):
    return [
        (place(z, y, c), place(z + (dist if c == 0 else -dist), y, c))
        for z in range(NZ) for y in range(NY) for c in range(NC)
    ]


def swap(k):
    return [(f, f ^ k) for f in range(NZ * NG)]


def z_groups():
    return [[place(z, y, c) for z in range(NZ)] for y in range(NY) for c in range(NC)]


def x_groups():
    return [[x * NR + y for x in range(NX)] for y in range(NR)]


def y_groups():
    return [[x * NR + y for y in range(NR)] for x in range(NX)]


def owner(dist, k=0):
    me = lax.axis_index("fsdp")
    z = me // NG
    forward = 1 - 2 * ((me % NC) ^ (k % NC))
    return (z + forward * dist + NZ) % NZ


def column_of(i):
    first = 0 if i < len(EARLY) else KVH * HD
    return first + i * ROWS


def piece_of(tok, i, k):
    me = lax.axis_index("fsdp")
    block = owner(DIST[i], k) * NG + ((me % NG) ^ k)
    return tok.at[:, pl.ds(pl.multiple_of(block * ROWS, ROWS), ROWS)]


def copy_all(pairs, sems):
    copies = [pltpu.make_async_copy(src, dst, sems.at[n]) for n, (src, dst) in enumerate(pairs)]
    for copy in copies:
        copy.start()
    for copy in copies:
        copy.wait()


def pack_early_kernel(tok, cot, y_early, x_early, near, sems):
    pairs = []
    for out, k in ((y_early, 2), (x_early, 3), (near, 1)):
        for i in range(len(DIST) if k == 1 else len(EARLY)):
            pairs.append((piece_of(tok, i, k), out.at[:, pl.ds(column_of(i), ROWS)]))
        pairs.append((cot, out.at[:, pl.ds(SPLIT - KVH * HD, KVH * HD)]))
    copy_all(pairs, sems)


def pack_late_kernel(tok, cot, y_late, x_late, own, sems):
    pairs = []
    for out, k in ((y_late, 2), (x_late, 3)):
        for i in range(len(EARLY), len(DIST)):
            pairs.append((piece_of(tok, i, k), out.at[:, pl.ds(column_of(i) - SPLIT, ROWS)]))
    for i in range(len(DIST)):
        pairs.append((piece_of(tok, i, 0), own.at[:, pl.ds(column_of(i), ROWS)]))
    pairs.append((cot, own.at[:, pl.ds(SPLIT - KVH * HD, KVH * HD)]))
    copy_all(pairs, sems)


def pick_kernel(frag, w, picked, sems):
    pairs = []
    for k in range(2):
        src = w.at[:, pl.ds(pl.multiple_of(frag[k] * HD, HD), HD)]
        pairs += [(src, picked.at[n, :, pl.ds(k * HD, HD)]) for n in range(NX)]
    copy_all(pairs, sems)


def levels_of(x):
    top = jnp.max(jnp.abs(x), axis=0, keepdims=True)
    power = jnp.ceil(jnp.log2(jnp.maximum(top, 1e-30)))
    return jnp.round(x * (LEVELS * jnp.exp2(-power))).astype(jnp.int32).astype(jnp.int16), power


def encode(x, out):
    coded, power = levels_of(x)
    out[:ROWS, :] = coded
    out[ROWS:, :] = jnp.broadcast_to(power, (GROUP, x.shape[1])).astype(jnp.int32).astype(jnp.int16)


def encode_pair(x, y, out):
    coded_x, power_x = levels_of(x)
    coded_y, power_y = levels_of(y)
    out[:ROWS, :] = coded_x
    out[ROWS : 2 * ROWS, :] = coded_y
    half = (GROUP // 2, x.shape[1])
    powers = jnp.concatenate([jnp.broadcast_to(power_x, half), jnp.broadcast_to(power_y, half)], axis=0)
    out[2 * ROWS :, :] = powers.astype(jnp.int32).astype(jnp.int16)


def decode(ref, at=0, blocks=1):
    powers = ref[blocks * ROWS :, :].astype(jnp.int32).astype(F32)
    row = at * (GROUP // blocks)
    scale = jnp.exp2(powers[row : row + 1]) * (1.0 / LEVELS)
    return ref[at * ROWS : (at + 1) * ROWS, :].astype(jnp.int32).astype(F32) * scale


def partial_grad(refs, cot, dist):
    columns = [block_of(first, second, DIST.index(dist)) for first, second in refs]
    features = jnp.concatenate(columns, axis=0)
    return lax.dot_general(features, cot, (((0,), (0,)), ((), ())), preferred_element_type=F32)


def block_of(first, second, i):
    at = column_of(i)
    if second is None or at < SPLIT:
        return first[:, at : at + ROWS]
    return second[:, at - SPLIT : at - SPLIT + ROWS]


def cotangents(refs):
    return jnp.concatenate([r[:, SPLIT - KVH * HD : SPLIT] for r, _ in refs], axis=0)


def early_kernel(own, near, y_early, x_early, far, ahead, behind):
    refs = [(r, None) for r in (own, near, y_early, x_early)]
    cot = cotangents(refs)
    encode(partial_grad(refs, cot, 4), far)
    encode_pair(partial_grad(refs, cot, 3), partial_grad(refs, cot, 1), ahead)
    encode_pair(partial_grad(refs, cot, -3), partial_grad(refs, cot, -1), behind)


def late_kernel(own, near, y_early, x_early, y_late, x_late, ahead2, behind2):
    refs = [(own, None), (near, None), (y_early, y_late), (x_early, x_late)]
    cot = cotangents(refs)
    ahead2[...] = partial_grad(refs, cot, 2)
    behind2[...] = partial_grad(refs, cot, -2)


def relay_kernel(mine_ahead, mine_behind, far, ahead, behind, ahead2, behind2):
    encode(mine_ahead[...] + decode(far) + decode(ahead, 0, 2), ahead2)
    encode(mine_behind[...] + decode(behind, 0, 2), behind2)


def key_kernel(own, near, y_early, x_early, y_late, x_late, w, moment, base, kept, sent):
    refs = [(own, None), (near, None), (y_early, y_late), (x_early, x_late)]
    for out, at, (first, second) in zip((kept, sent, kept, sent), (0, 0, TOK, TOK), refs):
        total = jnp.zeros((TOK, KVH * HD), F32)
        for i, dist in enumerate(DIST):
            rows = w[pl.ds(pl.multiple_of(owner(dist) * ROWS, ROWS), ROWS), :]
            total = total + jnp.dot(block_of(first, second, i), rows, preferred_element_type=F32)
        out[at : at + TOK, :] = total
    base[...] = BETA_INNER * moment[...] + partial_grad(refs, cotangents(refs), 0) * (D ** -0.5)


def picked_sum_kernel(picked, out):
    total = picked[0].astype(F32)
    for n in range(1, NX):
        total = total + picked[n].astype(F32)
    encode(total, out.at[0])
    for n in range(1, NR):
        out[n] = out[0]


def outer_kernel(sums, gf, om, global_new, outer_new, blend, *, replicas):
    total = decode(sums.at[0])
    for n in range(1, NR):
        total = total + decode(sums.at[n])
    for k in range(2):
        mean = gf[k] - total[:, k * HD : (k + 1) * HD] * (1.0 / replicas)
        out = MU_OUTER * om[k] + mean
        outer_new[k] = out
        new = gf[k] - LR_OUTER * (MU_OUTER * out + mean)
        global_new[k] = new
        blend[k] = (1.0 - ALPHA_MIX) * new


def update_kernel(frag, base, ahead2, behind2, ahead, behind, w, blend, moment_new, weight_new):
    others = decode(ahead2) + decode(behind2) + decode(ahead, 1, 2) + decode(behind, 1, 2)
    new = base[...] + others * (D ** -0.5)
    moment_new[...] = new
    inner = w[...].astype(F32) - LR_INNER * new
    for h in range(KVH):
        mine = inner[:, h * HD : (h + 1) * HD]
        first = ALPHA_MIX * mine + blend[0]
        second = ALPHA_MIX * mine + blend[1]
        merged = jnp.where(frag[0] == h, first, jnp.where(frag[1] == h, second, mine))
        weight_new[:, h * HD : (h + 1) * HD] = merged.astype(BF16)


def key_half_kernel(kept, got, mine, theirs):
    mine[...] = kept[:TOK, :] + got[:TOK, :]
    theirs[...] = kept[TOK:, :] + got[TOK:, :]


def key_sum_kernel(mine, got, out):
    out[...] = ((mine[...] + got[...]) * (D ** -0.5)).astype(BF16)


def call(kernel, outs, *args, scalars=0, copies=0, hint=0, first=False, narrow=0):
    space = pl.ANY if copies else pltpu.VMEM
    specs = [pl.BlockSpec(memory_space=pltpu.SMEM)] * scalars
    specs += [pl.BlockSpec(memory_space=space)] * (len(args) - scalars)
    for n in range(narrow):
        specs[n] = pl.BlockSpec((TOK, SPLIT), lambda i: (0, 0))
    return pl.pallas_call(
        kernel,
        grid=(1,) if narrow else (),
        out_shape=list(outs),
        in_specs=specs,
        out_specs=[pl.BlockSpec(memory_space=pltpu.VMEM)] * len(outs),
        scratch_shapes=[pltpu.SemaphoreType.DMA((copies,))] if copies else [],
        compiler_params=None if first else pltpu.CompilerParams(vmem_limit_bytes=16 * 2**20),
        cost_estimate=pl.CostEstimate(flops=hint * 10**9, bytes_accessed=0, transcendentals=0),
    )(*args)


def shape(*dims, kind=BF16):
    return jax.ShapeDtypeStruct(dims, kind)


def shards(tokens, cotangent, weight, moment, global_frag, outer_moment, fragment):
    replicas = lax.axis_size("rep")
    width = KVH * HD
    w = weight[0]
    w_rows = lax.all_gather(w, "fsdp", axis_index_groups=z_groups(), tiled=True)

    send = lambda x, pairs: lax.ppermute(x, "fsdp", pairs)
    y_early, x_early, near = call(
        pack_early_kernel, [shape(TOK, SPLIT)] * 2 + [shape(TOK, WIDE)], tokens[0], cotangent[0],
        copies=2 * len(EARLY) + len(DIST) + 3, first=True,
    )
    y_early = send(y_early, swap(2))
    x_early = send(x_early, swap(3))
    near = send(near, swap(1))
    (picked,) = call(pick_kernel, [shape(NX, ROWS, 2 * HD)], fragment, w, scalars=1, copies=2 * NX)
    y_late, x_late, own = call(
        pack_late_kernel, [shape(TOK, WIDE - SPLIT)] * 2 + [shape(TOK, WIDE)],
        tokens[0], cotangent[0], copies=2 * len(LATE) + len(DIST) + 1,
    )
    y_late = send(y_late, swap(2))
    x_late = send(x_late, swap(3))

    picked = lax.all_to_all(picked, "rep", 0, 0, axis_index_groups=x_groups())

    one = shape(CODED, width, kind=jnp.int16)
    two = shape(2 * ROWS + GROUP, width, kind=jnp.int16)
    wide = shape(ROWS, width, kind=F32)
    far, ahead, behind = call(early_kernel, [one, two, two], own, near, y_early, x_early, narrow=2)
    far, y_late = lax.optimization_barrier((far, y_late))
    far = send(far, ring(2))
    ahead = send(ahead, ring(1))
    behind = send(behind, ring(-1))
    got = (own, near, y_early, x_early, y_late, x_late)
    mine = call(late_kernel, [wide] * 2, *got, hint=14)
    (sums,) = call(picked_sum_kernel, [shape(NR, CODED, 2 * HD, kind=jnp.int16)], picked)
    sums = lax.all_to_all(sums, "rep", 0, 0, axis_index_groups=y_groups())
    outer = shape(2, ROWS, HD, kind=F32)
    global_new, outer_new, blend = call(
        functools.partial(outer_kernel, replicas=replicas), [outer] * 3, sums, global_frag, outer_moment
    )
    pair = shape(2 * TOK, width, kind=F32)
    base, kept, sent = call(key_kernel, [wide, pair, pair], *got, w_rows, moment[0])
    half = shape(TOK, width, kind=F32)
    mine_key, theirs_key = call(key_half_kernel, [half] * 2, kept, send(sent, swap(1)))
    base, far = lax.optimization_barrier((base, far))
    ahead2, behind2 = call(relay_kernel, [one] * 2, *mine, far, ahead, behind, hint=12)
    ahead2 = send(ahead2, ring(2))
    behind2 = send(behind2, ring(-2))
    (key_out,) = call(key_sum_kernel, [shape(TOK, width)], mine_key, send(theirs_key, swap(2)))

    moment_new, weight_new = call(
        update_kernel, [wide, shape(ROWS, width)],
        fragment, base, ahead2, behind2, ahead, behind, w, blend, scalars=1,
    )
    return key_out[None], moment_new[None], weight_new[None], global_new, outer_new


def solution(mesh):
    in_specs = (
        P("rep", "fsdp", None),
        P("rep", "fsdp", None),
        P("rep", "fsdp", None),
        P("rep", "fsdp", None),
        P(None, "fsdp", None),
        P(None, "fsdp", None),
        P(),
    )
    out_specs = (
        P("rep", "fsdp", None),
        P("rep", "fsdp", None),
        P("rep", "fsdp", None),
        P(None, "fsdp", None),
        P(None, "fsdp", None),
    )
    return jax.shard_map(shards, mesh=mesh, in_specs=in_specs, out_specs=out_specs, check_vma=False)
```
